32 devices in a mesh: col: 16 (over z, y, core), row: 2 (over x).
Axes of the slice: x: 2, y: 2, z: 4, core: 2. Of those that a mesh axis runs over, the one named last changes fastest.
Arguments:
- diag_blocks: float32 [32, 512, 512], P('col'), may hold values from -1 to 3, as said below
- panel_blocks: float32 [32, 8, 512, 512], P('col', None, 'row'), may hold values from -0.3 to 0.3
- ancestors: int32 [32, 8], P('col'), may hold values from 0 to 15, all different within a row; in each aligned block of 2 rows (0 to 1, 2 to 3, ...) at most 2 rows name the same one
- target_ids: int32 [16], P('col'), may hold values from 0 to 15, each once
- target_tiles: float32 [16, 512, 512], P('col', 'row'), may hold values from -6 to 6
Outputs:
- panel_factor: float32 [32, 8, 512, 512], P('col', None, 'row')
- updated_tiles: float32 [16, 512, 512], P('col', 'row')
The draws below stay inside these ranges and needn't reach their ends.
Inputs may be any that keep to these rules, and one draw needn't show every extreme that they name: `ancestors`: each row names 8 different target blocks; on the supernodes of one index of col a target block is named at most twice, and exactly twice somewhere; every target block is named. `target_ids`: A permutation of the target blocks. `diag_blocks`: each block is symmetric and positive definite, with smallest eigenvalue 0.05 or more.
All inputs are finite; a program needn't handle non-finite values.
Results may differ from the reference program's by a relative error of at most 0.0029.
Values may be sent and summed in bfloat16 or wider, within the bound.
A program may use at most 128 MiB of HBM per device.

```python
import math
import jax
import jax.numpy as jnp
import numpy as np
from jax import lax

W = 512
ANC = 8
SN_DEV = 2
NS = 32
NT = 16


def gram_block(mixing, shift):
    gram = jnp.dot(mixing, mixing.T, precision=lax.Precision.HIGHEST) * (0.5 / W)
    gram = 0.5 * (gram + gram.T)
    return gram + shift * jnp.eye(W, dtype=jnp.float32)


def draw_diag_blocks(key, part):
    key = jax.random.fold_in(key, 11)
    key_mix, key_shift = jax.random.split(key)
    block_keys = jax.random.split(key_mix, NS)
    shifts = jnp.exp(jax.random.uniform(key_shift, (NS,), jnp.float32, math.log(0.1), math.log(0.5)))

    def one_block(args):
        block_key, shift = args
        mixing = jax.random.truncated_normal(block_key, -4.0, 4.0, (W, 2 * W), jnp.float32)
        return gram_block(mixing, shift)
    return lax.map(one_block, (block_keys, shifts)).astype(jnp.float32)


def block_levels(rng, shape, shards, low, top_value):
    loudness, own = 1.0, jax.random.fold_in(rng, 6)
    for axis_at, shards_of in shards:
        draws = jnp.exp(jax.random.uniform(jax.random.fold_in(own, axis_at), (shards_of,), jnp.float32, low / len(shards), top_value / len(shards)))
        loudness = loudness * jnp.repeat(draws, shape[axis_at] // shards_of).reshape([-1 if axis == axis_at else 1 for axis in range(len(shape))])
    return loudness


def shared_out(rng, own, number, rows, number_of, top, limit, slope):
    sequence = jax.random.permutation(rng, number_of)
    crowded, ordinary = shares(number_of, rows * top, limit, slope, True), shares(number_of, rows * top, limit, slope, False)
    places = jnp.arange(number_of)

    def named(lengths, offset_by):
        used = int((lengths > 0).sum())
        fixed = max(1, used // 4)
        moved = fixed + (places - fixed + offset_by * (used - fixed)) % max(1, number_of - fixed)
        return jnp.zeros((number_of,), jnp.int32).at[sequence[jnp.where(places < fixed, places, moved)]].set(jnp.asarray(lengths, jnp.int32))

    lengths = jnp.where(number % 4 == 0, named(crowded, number // 4), named(ordinary, number - number // 4 - 1))
    mixed = jax.random.permutation(jax.random.fold_in(own, 3), number_of)
    giver, sink = mixed[0:number_of // 2 * 2:2], mixed[1:number_of // 2 * 2:2]
    margin = jnp.minimum(lengths[giver] - 1, limit - lengths[sink]) // 2
    margin = jnp.where((giver == sequence[0]) | (sink == sequence[0]) | (lengths[sink] == 0), 0, jnp.maximum(margin, 0))
    moved = jax.random.randint(jax.random.fold_in(own, 4), (number_of // 2,), 0, 1 << 20) % (margin + 1)
    lengths = lengths.at[giver].add(-moved).at[sink].add(moved)
    items = jnp.searchsorted(jnp.cumsum(lengths), jnp.arange(rows * top), side="right").astype(jnp.int32)
    table = items.reshape(top, rows).T
    table = table[jax.random.permutation(jax.random.fold_in(own, 1), rows)]
    offset_by = jax.random.randint(jax.random.fold_in(own, 2), (rows, 1), 0, top)
    return jnp.take_along_axis(table, (jnp.arange(top)[None, :] + offset_by) % top, axis=1)


def shares(amount, total, bound, slope, full):
    loads = [(1 << 20) // math.isqrt(rank ** slope) + 1 for rank in range(1, amount + 1)]
    largest = bound if full else min(bound, max(-(-total // amount), total * loads[0] // sum(loads)))
    least = 1 if total - largest >= amount - 1 else 0
    holding, rest = [largest] + [least] * (amount - 1), total - largest - least * (amount - 1)
    while rest > 0:
        free = [i for i in range(1, amount) if holding[i] < largest] or [i for i in range(1, amount) if holding[i] < bound]
        whole, left = sum([loads[i] for i in free]), rest
        for i in free:
            extra = min(bound - holding[i], max(1, left * loads[i] // whole), rest)
            holding[i] = holding[i] + extra
            rest = rest - extra
    return np.array(holding)


def normal_values(stream_key, dims, width, bound, cuts=(), kind=jnp.bfloat16):
    gain = block_levels(stream_key, dims, cuts, -0.22, 0.18) if cuts else 1.0
    values = jax.random.normal(stream_key, dims, jnp.float32) * width * gain
    return jnp.minimum(jnp.maximum(values, -bound), bound).astype(kind)


def setup_inputs(seed: int = 0) -> dict:
    seeds = jax.random.split(jax.random.key(seed), 6)
    diag_blocks = draw_diag_blocks(jax.random.fold_in(seeds[5], 71), 0)
    panel_blocks = normal_values(seeds[1], (NS, ANC, W, W), 0.05, 0.3, ((0, 16), (2, 2)), jnp.float32)
    ancestors_keys = jax.random.split(jax.random.fold_in(seeds[2], 1), NS // SN_DEV)
    ancestors_turns = jax.random.permutation(jax.random.fold_in(seeds[2], 3), NS // SN_DEV)
    ancestors = jax.vmap(lambda own, number: shared_out(jax.random.fold_in(seeds[2], 2), own, number, SN_DEV, NT, ANC, 2, 2))(ancestors_keys, ancestors_turns).reshape((NS, ANC))
    target_ids = jax.random.permutation(seeds[3], NT).astype(jnp.int32)
    target_tiles = normal_values(seeds[4], (NT, W, W), 1.0, 6.0, ((0, 16), (1, 2)), jnp.float32)
    return dict(diag_blocks=diag_blocks, panel_blocks=panel_blocks, ancestors=ancestors, target_ids=target_ids, target_tiles=target_tiles)


def solve_panel(args):
    diag_block, panel = args
    factor = jnp.linalg.cholesky(diag_block)
    rhs = jnp.swapaxes(panel.reshape(ANC * W, W), 0, 1)
    solved = jax.scipy.linalg.solve_triangular(factor, rhs, lower=True)
    return jnp.swapaxes(solved, 0, 1).reshape(ANC, W, W)

def reference(diag_blocks, panel_blocks, ancestors, target_ids, target_tiles):
    panel_factor = lax.map(solve_panel, (diag_blocks, panel_blocks))
    rounded = panel_factor.astype(jnp.bfloat16)
    matches = ancestors[:, :, None] == target_ids[None, None, :]
    position = jnp.sum(jnp.where(matches, jnp.arange(NT, dtype=jnp.int32)[None, None, :], 0), axis=2).astype(jnp.int32)
    flat_pos = position.reshape(NS * ANC)

    def accumulate(index, total):
        s_idx = index // ANC
        j_idx = index % ANC
        tile = rounded[s_idx, j_idx]
        product = jnp.dot(tile.astype(jnp.float32), tile.T.astype(jnp.float32), preferred_element_type=jnp.float32)
        return total.at[flat_pos[index]].add(product)
    update = lax.fori_loop(0, NS * ANC, accumulate, jnp.zeros((NT, W, W), jnp.float32))
    return (panel_factor, target_tiles - update)
```

```python
import functools

import jax
import jax.numpy as jnp
from jax import lax
from jax.experimental import pallas as pl
from jax.experimental.pallas import tpu as pltpu
from jax.sharding import PartitionSpec as P

NB = 128
F32 = jnp.float32
BF16 = jnp.bfloat16


def dot_exact(a, b):
    return jnp.dot(a, b, preferred_element_type=F32, precision=lax.Precision.HIGHEST)


def eliminate(blocks, frozen):
    count = len(blocks)
    lane = lax.broadcasted_iota(jnp.int32, (1, NB), 1)
    sub = lax.broadcasted_iota(jnp.int32, (8, NB), 0)
    head = [None] * count
    tail = list(blocks)
    for g in range(NB // 8):
        rows = NB - 8 * g - 8
        cols_head, cols_tail = [], []
        for s in range(count):
            a = tail[s]
            head[s], tail[s] = a[:8], (a[8:] if rows else None)
            cols_head.append(
                [jnp.broadcast_to(head[s][:, 8 * g + m : 8 * g + m + 1], (8, NB)) for m in range(8)]
            )
            cols_tail.append(
                [jnp.broadcast_to(tail[s][:, 8 * g + m : 8 * g + m + 1], (rows, NB)) for m in range(8)]
                if rows
                else None
            )
        for k in range(8):
            at = lane == 8 * g + k
            for s in range(count):
                ch, ct = cols_head[s], cols_tail[s]
                inv = lax.rsqrt(ch[k][k : k + 1, :])
                recip = inv * inv
                row = head[s][k : k + 1, :]
                frozen[s, 8 * g + k : 8 * g + k + 1, :] = jnp.where(at, inv, row * inv)
                step = jnp.where(at, 1.0 + recip, row * recip)
                below = jnp.where(sub > k, ch[k], 0.0)
                head[s] = head[s] - below * step
                if rows:
                    tail[s] = tail[s] - ct[k] * step
                for m in range(k + 1, 8):
                    scale = ch[m][k : k + 1, :] * recip
                    ch[m] = ch[m] - below * scale
                    if rows:
                        ct[m] = ct[m] - ct[k] * scale


def factor_kernel(diag_ref, hi_ref, lo_ref, work, frozen):
    count, width, _ = diag_ref.shape
    work[...] = diag_ref[...]
    lower = lax.broadcasted_iota(jnp.int32, (NB, NB), 0) >= lax.broadcasted_iota(
        jnp.int32, (NB, NB), 1
    )
    lane_block = lax.broadcasted_iota(jnp.int32, (1, width), 1) // NB

    def block_step(b, carry):
        here = pl.ds(pl.multiple_of(b * NB, NB), NB)
        eliminate([work[s, here, here] for s in range(count)], frozen)
        own = lane_block == b
        for s in range(count):
            inverse = jnp.where(lower, frozen[s], 0.0)
            work[s, here, :] = dot_exact(inverse, work[s, here, :])
            work[s, here, here] = inverse

        def trailing(i, carry):
            there = pl.ds(pl.multiple_of(i * NB, NB), NB)
            for s in range(count):
                left = work[s, here, there].T
                old = jnp.where(own, 0.0, work[s, there, :])
                work[s, there, :] = old - dot_exact(left, work[s, here, :])
            return carry

        return lax.fori_loop(b + 1, width // NB, trailing, carry)

    lax.fori_loop(0, width // NB, block_step, 0)
    keep = lax.broadcasted_iota(jnp.int32, (width, width), 0) >= lax.broadcasted_iota(
        jnp.int32, (width, width), 1
    )
    for s in range(count):
        inverse = jnp.where(keep, work[s], 0.0).T
        hi = inverse.astype(BF16)
        hi_ref[s] = hi
        lo_ref[s] = (inverse - hi.astype(F32)).astype(BF16)


def inverse_factors(diag_blocks):
    count, width, _ = diag_blocks.shape
    out = jax.ShapeDtypeStruct((count, width, width), BF16)
    return pl.pallas_call(
        factor_kernel,
        out_shape=(out, out),
        in_specs=[pl.BlockSpec(memory_space=pltpu.VMEM)],
        out_specs=(pl.BlockSpec(memory_space=pltpu.VMEM),) * 2,
        scratch_shapes=[
            pltpu.VMEM((count, width, width), F32),
            pltpu.VMEM((count, NB, NB), F32),
        ],
        compiler_params=pltpu.CompilerParams(vmem_limit_bytes=40 * 2**20),
        cost_estimate=pl.CostEstimate(
            flops=40 * 10**9, bytes_accessed=4 * count * width * width, transcendentals=0
        ),
        name="factor",
    )(diag_blocks)


def dot_nt(a, b):
    return lax.dot_general(a, b, (((1,), (1,)), ((), ())), preferred_element_type=F32)


def place_tile(tile, slot, keep_ref, send_ref):
    half = keep_ref.shape[0]

    @pl.when(slot < half)
    def _():
        keep_ref[slot] = tile(keep_ref[slot])

    @pl.when(slot >= half)
    def _():
        send_ref[slot - half] = tile(send_ref[slot - half])


def panel_kernel(
    slot_ref, mine_ref, panel_ref, other_ref, hi_ref, lo_ref,
    out_ref, same_keep, same_send, cross_keep, cross_send,
):
    s, j = pl.program_id(0), pl.program_id(1)
    blocks, rows, width = panel_ref.shape[1:]
    low = width // 2

    @pl.when((s == 0) & (j == 0))
    def _():
        for ref in (same_keep, same_send, cross_keep, cross_send):
            ref[...] = jnp.zeros_like(ref)

    def times_inverse(lhs, factor):
        left = jnp.dot(lhs[:, :low], factor[:low, :low], preferred_element_type=F32)
        right = jnp.dot(lhs, factor[:, low:], preferred_element_type=F32)
        return jnp.concatenate([left, right], axis=1)

    hi, lo = hi_ref[0], lo_ref[0]
    rhs = panel_ref[0].reshape(blocks * rows, width)
    rhs_hi = rhs.astype(BF16)
    rhs_lo = (rhs - rhs_hi.astype(F32)).astype(BF16)
    solved = times_inverse(rhs_hi, hi) + times_inverse(rhs_lo, hi) + times_inverse(rhs_hi, lo)
    out_ref[0] = solved.reshape(blocks, rows, width)
    rounded = solved.astype(BF16).reshape(blocks, rows, width)
    diagonal = lax.broadcasted_iota(jnp.int32, (rows, rows), 0) == lax.broadcasted_iota(
        jnp.int32, (rows, rows), 1
    )
    extra = lax.broadcasted_iota(jnp.int32, (16, rows), 0)
    for i in range(blocks):
        product = dot_nt(rounded[i], rounded[i])
        sums = jnp.sum(jnp.where(diagonal, product, 0.0), axis=0, keepdims=True)
        product = jnp.where(diagonal, 0.0, product)

        def added(old):
            tail = old[rows:].astype(F32)
            total = jnp.sum(tail, axis=0, keepdims=True) + sums
            top = total.astype(BF16).astype(F32)
            rest = jnp.where(extra == 0, top, jnp.where(extra == 1, total - top, 0.0))
            return jnp.concatenate([old[:rows].astype(F32) + product, rest], axis=0).astype(BF16)

        place_tile(added, slot_ref[s, j * blocks + i], same_keep, same_send)

    @pl.when(s == mine_ref[0])
    def _():
        got = other_ref[...].reshape(blocks * rows, width)
        partner = (times_inverse(got, hi) + times_inverse(got, lo)).astype(BF16)
        partner = partner.reshape(blocks, rows, width)
        for i in range(blocks):
            product = dot_nt(rounded[i], partner[i]).astype(BF16)
            place_tile(lambda old: product, slot_ref[s, j * blocks + i], cross_keep, cross_send)


def panel_products(slot, mine, panel_blocks, other, hi, lo, targets):
    count, blocks, rows, width = panel_blocks.shape
    step = 2 if blocks % 2 == 0 else 1
    steps = blocks // step
    shapes = [(targets // 2, rows + 16, rows)] * 2 + [(targets // 2, rows, rows)] * 2
    whole = [pl.BlockSpec(shape, lambda s, j, slot, mine: (0, 0, 0)) for shape in shapes]
    factor = pl.BlockSpec((1, width, width), lambda s, j, slot, mine: (s, 0, 0))
    panel = pl.BlockSpec((1, step, rows, width), lambda s, j, slot, mine: (s, j, 0, 0))

    def other_at(s, j, slot, mine):
        return (jnp.where(s == mine[0], j, jnp.where(s < mine[0], 0, steps - 1)), 0, 0)

    return pl.pallas_call(
        panel_kernel,
        out_shape=[jax.ShapeDtypeStruct(panel_blocks.shape, F32)]
        + [jax.ShapeDtypeStruct(shape, BF16) for shape in shapes],
        grid_spec=pltpu.PrefetchScalarGridSpec(
            num_scalar_prefetch=2,
            grid=(count, steps),
            in_specs=[panel, pl.BlockSpec((step, rows, width), other_at), factor, factor],
            out_specs=[panel] + whole,
        ),
        compiler_params=pltpu.CompilerParams(
            vmem_limit_bytes=56 * 2**20, dimension_semantics=("arbitrary", "arbitrary")
        ),
        name="panel",
    )(slot, mine, panel_blocks, other, hi, lo)


def packed(value, rows):
    if value.shape[-2] == rows:
        return value.astype(BF16)
    total = value[..., rows : rows + 1, :] + value[..., rows + 1 : rows + 2, :]
    top = lax.reduce_precision(total, 8, 7)
    row = lax.broadcasted_iota(jnp.int32, value.shape, value.ndim - 2)
    value = jnp.where(row == rows, top, jnp.where(row == rows + 1, total - top, value))
    return value.astype(BF16)


def halve_and_add(keep, send, order, columns, rows):
    shape = keep.shape[1:]
    for step, bit in enumerate(order):
        got = lax.ppermute(send, "col", [(c, c ^ (1 << bit)) for c in range(columns)])
        value = keep.astype(F32) + got.astype(F32)
        half = value.shape[0] // 2
        if half:
            keep, send = value[:half], packed(value[half:], rows)
    return value.reshape(shape)


def gathered(slot, panel_blocks, hi, lo, columns):
    count, blocks, rows, width = panel_blocks.shape
    inverse = hi.astype(F32) + lo.astype(F32)
    solved = jnp.einsum("sjaw,swv->sjav", panel_blocks, inverse, precision=lax.Precision.HIGHEST)
    rounded = solved.astype(BF16)
    tiles = jnp.zeros((columns, rows, width), F32)
    for s in range(count):
        full = lax.all_gather(rounded[s], "row", axis=1, tiled=True)
        products = jnp.einsum("jaw,jbw->jab", rounded[s], full, preferred_element_type=F32)
        tiles = tiles.at[slot[s]].add(products)
    return solved, tiles


def on_device(columns, halves, diag_blocks, panel_blocks, ancestors, target_ids, target_tiles):
    me, half = lax.axis_index("col"), lax.axis_index("row")
    paired = halves == 2 and panel_blocks.shape[0] == 2
    swap = [(0, 1), (1, 0)]
    if paired:
        outgoing = lax.dynamic_index_in_dim(panel_blocks, 1 - half, 0, keepdims=False).astype(BF16)
        other = lax.ppermute(outgoing, "row", swap)
    spread = lax.optimization_barrier(jnp.broadcast_to(target_ids, (8, 128)))
    all_ids = lax.optimization_barrier(lax.all_gather(spread, "col", axis=0, tiled=True))
    all_ids = all_ids.reshape(columns, 8, 128)[:, 0, 0]
    matches = ancestors[:, :, None] == all_ids[None, None, :]
    place = jnp.arange(columns, dtype=jnp.int32)
    position = jnp.sum(jnp.where(matches, place[None, None, :], 0), axis=2)
    distance = (position ^ me).astype(jnp.int32)
    bits = list(range(columns.bit_length() - 1))
    slot = jnp.zeros_like(distance)
    for bit in bits:
        slot = slot * 2 + ((distance >> bit) & 1)
    hi, lo = inverse_factors(diag_blocks)
    if not paired:
        panel_factor, tiles = gathered(slot, panel_blocks, hi, lo, columns)
        rows = tiles.shape[1]
        keep, send = tiles[: columns // 2], tiles[columns // 2 :].astype(BF16)
        return (panel_factor, target_tiles - halve_and_add(keep, send, bits, columns, rows)[None])
    mine = half.astype(jnp.int32).reshape(1)
    panel_factor, same_keep, same_send, cross_keep, cross_send = panel_products(
        slot, mine, panel_blocks, other, hi, lo, columns
    )
    rows = panel_blocks.shape[2]
    same = halve_and_add(same_keep, same_send, bits, columns, rows)
    diagonal = same[rows : rows + 1] + same[rows + 1 : rows + 2]
    same = same[:rows] + jnp.where(jnp.eye(rows, dtype=bool), diagonal, 0.0)
    cross = halve_and_add(cross_keep, cross_send, bits, columns, rows)
    back = lax.ppermute(cross.astype(BF16), "row", swap)
    cross = cross + back.astype(F32).T
    update = jnp.where(
        half == 0,
        jnp.concatenate([same, cross], axis=1),
        jnp.concatenate([cross, same], axis=1),
    )
    return (panel_factor, target_tiles - update[None])


def solution(mesh):
    in_specs = (
        P("col", None, None),
        P("col", None, "row", None),
        P("col", None),
        P("col"),
        P("col", "row", None),
    )
    out_specs = (P("col", None, "row", None), P("col", "row", None))
    return jax.shard_map(
        functools.partial(on_device, mesh.shape["col"], mesh.shape["row"]),
        mesh=mesh,
        in_specs=in_specs,
        out_specs=out_specs,
        check_vma=False,
    )
```

```python
import functools

import jax
import jax.numpy as jnp
from jax import lax
from jax.experimental import pallas as pl
from jax.experimental.pallas import tpu as pltpu
from jax.sharding import PartitionSpec as P

NB = 128
F32 = jnp.float32
BF16 = jnp.bfloat16


def dot_exact(a, b):
    return jnp.dot(a, b, preferred_element_type=F32, precision=lax.Precision.HIGHEST)


def eliminate(blocks, frozen):
    count = len(blocks)
    lane = lax.broadcasted_iota(jnp.int32, (1, NB), 1)
    sub = lax.broadcasted_iota(jnp.int32, (8, NB), 0)
    head = [None] * count
    tail = list(blocks)
    for g in range(NB // 8):
        rows = NB - 8 * g - 8
        cols_head, cols_tail = [], []
        for s in range(count):
            a = tail[s]
            head[s], tail[s] = a[:8], (a[8:] if rows else None)
            cols_head.append(
                [jnp.broadcast_to(head[s][:, 8 * g + m : 8 * g + m + 1], (8, NB)) for m in range(8)]
            )
            cols_tail.append(
                [jnp.broadcast_to(tail[s][:, 8 * g + m : 8 * g + m + 1], (rows, NB)) for m in range(8)]
                if rows
                else None
            )
        for k in range(8):
            at = lane == 8 * g + k
            for s in range(count):
                ch, ct = cols_head[s], cols_tail[s]
                inv = lax.rsqrt(ch[k][k : k + 1, :])
                recip = inv * inv
                row = head[s][k : k + 1, :]
                frozen[s, 8 * g + k : 8 * g + k + 1, :] = jnp.where(at, inv, row * inv)
                step = jnp.where(at, 1.0 + recip, row * recip)
                below = jnp.where(sub > k, ch[k], 0.0)
                head[s] = head[s] - below * step
                if rows:
                    tail[s] = tail[s] - ct[k] * step
                for m in range(k + 1, 8):
                    scale = ch[m][k : k + 1, :] * recip
                    ch[m] = ch[m] - below * scale
                    if rows:
                        ct[m] = ct[m] - ct[k] * scale


def factor_kernel(diag_ref, hi_ref, lo_ref, work, frozen):
    count, width, _ = diag_ref.shape
    work[...] = diag_ref[...]
    lower = lax.broadcasted_iota(jnp.int32, (NB, NB), 0) >= lax.broadcasted_iota(
        jnp.int32, (NB, NB), 1
    )
    lane_block = lax.broadcasted_iota(jnp.int32, (1, width), 1) // NB

    def block_step(b, carry):
        here = pl.ds(pl.multiple_of(b * NB, NB), NB)
        eliminate([work[s, here, here] for s in range(count)], frozen)
        own = lane_block == b
        for s in range(count):
            inverse = jnp.where(lower, frozen[s], 0.0)
            work[s, here, :] = dot_exact(inverse, work[s, here, :])
            work[s, here, here] = inverse

        def trailing(i, carry):
            there = pl.ds(pl.multiple_of(i * NB, NB), NB)
            for s in range(count):
                left = work[s, here, there].T
                old = jnp.where(own, 0.0, work[s, there, :])
                work[s, there, :] = old - dot_exact(left, work[s, here, :])
            return carry

        return lax.fori_loop(b + 1, width // NB, trailing, carry)

    lax.fori_loop(0, width // NB, block_step, 0)
    keep = lax.broadcasted_iota(jnp.int32, (width, width), 0) >= lax.broadcasted_iota(
        jnp.int32, (width, width), 1
    )
    for s in range(count):
        inverse = jnp.where(keep, work[s], 0.0).T
        hi = inverse.astype(BF16)
        hi_ref[s] = hi
        lo_ref[s] = (inverse - hi.astype(F32)).astype(BF16)


def inverse_factors(diag_blocks):
    count, width, _ = diag_blocks.shape
    out = jax.ShapeDtypeStruct((count, width, width), BF16)
    return pl.pallas_call(
        factor_kernel,
        out_shape=(out, out),
        in_specs=[pl.BlockSpec(memory_space=pltpu.VMEM)],
        out_specs=(pl.BlockSpec(memory_space=pltpu.VMEM),) * 2,
        scratch_shapes=[
            pltpu.VMEM((count, width, width), F32),
            pltpu.VMEM((count, NB, NB), F32),
        ],
        compiler_params=pltpu.CompilerParams(vmem_limit_bytes=40 * 2**20),
        cost_estimate=pl.CostEstimate(
            flops=40 * 10**9, bytes_accessed=4 * count * width * width, transcendentals=0
        ),
        name="factor",
    )(diag_blocks)


def dot_nt(a, b):
    return lax.dot_general(a, b, (((1,), (1,)), ((), ())), preferred_element_type=F32)


def split_diagonal(tail, first, second, extra):
    rest = 0.0
    for at, term in ((0, first), (2, second)):
        total = tail[at : at + 1] + tail[at + 1 : at + 2] + term
        top = total.astype(BF16).astype(F32)
        rest = jnp.where(extra == at, top, jnp.where(extra == at + 1, total - top, rest))
    return rest


def place_tile(tile, slot, keep_ref, send_ref):
    half = keep_ref.shape[0]

    @pl.when(slot < half)
    def _():
        keep_ref[slot] = tile(keep_ref[slot])

    @pl.when(slot >= half)
    def _():
        send_ref[slot - half] = tile(send_ref[slot - half])


def panel_kernel(
    slot_ref, mine_ref, panel_ref, other_ref, hi_ref, lo_ref,
    out_ref, same_keep, same_send, cross_keep, cross_send,
):
    s, j = pl.program_id(0), pl.program_id(1)
    blocks, rows, width = panel_ref.shape[1:]
    low = width // 2

    @pl.when((s == 0) & (j == 0))
    def _():
        for ref in (same_keep, same_send, cross_keep, cross_send):
            ref[...] = jnp.zeros_like(ref)

    def times_inverse(lhs, factor):
        left = jnp.dot(lhs[:, :low], factor[:low, :low], preferred_element_type=F32)
        right = jnp.dot(lhs, factor[:, low:], preferred_element_type=F32)
        return jnp.concatenate([left, right], axis=1)

    hi, lo = hi_ref[0], lo_ref[0]
    rhs = panel_ref[0].reshape(blocks * rows, width)
    rhs_hi = rhs.astype(BF16)
    rhs_lo = (rhs - rhs_hi.astype(F32)).astype(BF16)
    solved = times_inverse(rhs_hi, hi) + times_inverse(rhs_lo, hi) + times_inverse(rhs_hi, lo)
    out_ref[0] = solved.reshape(blocks, rows, width)
    rounded = solved.astype(BF16).reshape(blocks, rows, width)
    diagonal = lax.broadcasted_iota(jnp.int32, (rows, rows), 0) == lax.broadcasted_iota(
        jnp.int32, (rows, rows), 1
    )
    extra = lax.broadcasted_iota(jnp.int32, (16, NB), 0)
    for i in range(blocks):
        product = dot_nt(rounded[i], rounded[i])
        sums = jnp.sum(jnp.where(diagonal, product, 0.0), axis=0, keepdims=True)
        product = jnp.where(diagonal, 0.0, product)
        lower = [product[:NB, :NB], product[NB:, :NB], product[NB:, NB:]]

        def added(old):
            rest = split_diagonal(old[3 * NB :].astype(F32), sums[:, :NB], sums[:, NB:], extra)
            return jnp.concatenate(
                [old[: 3 * NB].astype(F32) + jnp.concatenate(lower, axis=0), rest], axis=0
            ).astype(BF16)

        place_tile(added, slot_ref[s, j * blocks + i], same_keep, same_send)

    @pl.when(s == mine_ref[0])
    def _():
        got = other_ref[...].reshape(blocks * rows, width)
        partner = (times_inverse(got, hi) + times_inverse(got, lo)).astype(BF16)
        partner = partner.reshape(blocks, rows, width)
        for i in range(blocks):
            slot = slot_ref[s, j * blocks + i]
            first, second = rounded[i], partner[i]

            @pl.when(mine_ref[0] == 0)
            def _():
                product = dot_nt(first, second).astype(BF16)
                place_tile(lambda old: product, slot, cross_keep, cross_send)

            @pl.when(mine_ref[0] != 0)
            def _():
                product = dot_nt(second, first).astype(BF16)
                place_tile(lambda old: product, slot, cross_keep, cross_send)


def panel_products(slot, mine, panel_blocks, other, hi, lo, targets):
    count, blocks, rows, width = panel_blocks.shape
    step = 2 if blocks % 2 == 0 else 1
    steps = blocks // step
    shapes = [(targets // 2, 3 * NB + 16, NB)] * 2 + [(targets // 2, rows, rows)] * 2
    whole = [pl.BlockSpec(shape, lambda s, j, slot, mine: (0, 0, 0)) for shape in shapes]
    factor = pl.BlockSpec((1, width, width), lambda s, j, slot, mine: (s, 0, 0))
    panel = pl.BlockSpec((1, step, rows, width), lambda s, j, slot, mine: (s, j, 0, 0))

    def other_at(s, j, slot, mine):
        return (jnp.where(s == mine[0], j, jnp.where(s < mine[0], 0, steps - 1)), 0, 0)

    return pl.pallas_call(
        panel_kernel,
        out_shape=[jax.ShapeDtypeStruct(panel_blocks.shape, F32)]
        + [jax.ShapeDtypeStruct(shape, BF16) for shape in shapes],
        grid_spec=pltpu.PrefetchScalarGridSpec(
            num_scalar_prefetch=2,
            grid=(count, steps),
            in_specs=[panel, pl.BlockSpec((step, rows, width), other_at), factor, factor],
            out_specs=[panel] + whole,
        ),
        compiler_params=pltpu.CompilerParams(
            vmem_limit_bytes=56 * 2**20, dimension_semantics=("arbitrary", "arbitrary")
        ),
        name="panel",
    )(slot, mine, panel_blocks, other, hi, lo)


def halve_and_add(keep, send, order, columns):
    shape = keep.shape[1:]
    for bit in order:
        got = lax.ppermute(send, "col", [(c, c ^ (1 << bit)) for c in range(columns)])
        value = keep.astype(F32) + got.astype(F32)
        half = value.shape[0] // 2
        if half:
            keep, send = value[:half], value[half:].astype(BF16)
    return value.reshape(shape)


def flipped(index, bits):
    bit = 1
    other = index
    while bit <= bits:
        if bits & bit:
            other = other + bit * (1 - 2 * ((index // bit) % 2))
        bit *= 2
    return other


def meet(peers):
    barrier = pltpu.get_barrier_semaphore()
    for peer in peers:
        pl.semaphore_signal(barrier, inc=1, device_id=peer, device_id_type=pl.DeviceIdType.MESH)
    pl.semaphore_wait(barrier, len(peers))


def ids_kernel(own_ref, out_ref, landed, send_sem, recv_sem):
    columns = out_ref.shape[0]
    me, half = lax.axis_index("col"), lax.axis_index("row")
    peers = [(flipped(me, q), half) for q in range(1, columns)]
    meet(peers)
    copies = []
    for q in range(1, columns):
        copy = pltpu.make_async_remote_copy(
            src_ref=own_ref,
            dst_ref=landed.at[q],
            send_sem=send_sem.at[q],
            recv_sem=recv_sem.at[q],
            device_id=peers[q - 1],
            device_id_type=pl.DeviceIdType.MESH,
        )
        copy.start()
        copies.append(copy)
    out_ref[0] = own_ref[...]
    for q, copy in enumerate(copies, 1):
        copy.wait()
        out_ref[q] = landed[q]


def ids_by_distance(target_ids, columns):
    own = jnp.broadcast_to(target_ids, (8, 128))
    out = pl.pallas_call(
        ids_kernel,
        out_shape=jax.ShapeDtypeStruct((columns, 8, 128), jnp.int32),
        in_specs=[pl.BlockSpec(memory_space=pltpu.VMEM)],
        out_specs=pl.BlockSpec(memory_space=pltpu.VMEM),
        scratch_shapes=[
            pltpu.VMEM((columns, 8, 128), jnp.int32),
            pltpu.SemaphoreType.DMA((columns,)),
            pltpu.SemaphoreType.DMA((columns,)),
        ],
        compiler_params=pltpu.CompilerParams(collective_id=0, has_side_effects=True),
        name="ids",
    )(own)
    return out[:, 0, 0]


def reduce_kernel(
    order, same_keep, same_send, cross_keep, cross_send, target_ref, out_ref,
    same_acc, same_out, same_got, cross_acc, cross_out, cross_got0, cross_got,
    swap_out, swap_got, last_out, last_got, full, send_sem, recv_sem,
):
    me, half = lax.axis_index("col"), lax.axis_index("row")
    partner = (me, 1 - half)
    peers = [(flipped(me, 1 << bit), half) for bit in order]
    stages = len(order)
    rows = 2 * NB
    meet(peers + [partner])
    extra = lax.broadcasted_iota(jnp.int32, (16, NB), 0)
    kept_rows = pl.ds(pl.multiple_of(half * NB, NB), NB)
    sent_rows = pl.ds(pl.multiple_of((1 - half) * NB, NB), NB)
    count = same_keep.shape[0]
    sizes = [count >> t for t in range(stages)]
    starts = [sum(sizes[1:t]) for t in range(stages)]

    def remote(number, src, dst, device):
        copy = pltpu.make_async_remote_copy(
            src_ref=src,
            dst_ref=dst,
            send_sem=send_sem.at[number],
            recv_sem=recv_sem.at[number],
            device_id=device,
            device_id_type=pl.DeviceIdType.MESH,
        )
        copy.start()
        return copy

    def same_stage(t):
        size = sizes[t]
        base = 0 if t == 0 else count + starts[t]

        def total(q):
            mine = same_keep[q].astype(F32) if t == 0 else same_acc[q]
            return mine + same_got[base + q].astype(F32)

        if size == 1:
            same_acc[0] = total(0)
            return None
        send_at = starts[t + 1]

        def send_tile(i, carry):
            value = total(size // 2 + i)
            rest = split_diagonal(value[3 * NB :], 0.0, 0.0, extra)
            same_out[send_at + i] = jnp.concatenate([value[: 3 * NB], rest], axis=0).astype(BF16)
            return carry

        lax.fori_loop(0, size // 2, send_tile, 0)
        copy = remote(
            t + 1,
            same_out.at[pl.ds(send_at, size // 2)],
            same_got.at[pl.ds(count + send_at, size // 2)],
            peers[t + 1],
        )

        def keep_tile(q, carry):
            same_acc[q] = total(q)
            return carry

        lax.fori_loop(0, size // 2, keep_tile, 0)
        return copy

    def cross_first():
        def send_tile(q, carry):
            value = cross_keep[q, sent_rows, :].astype(F32) + cross_got0[q, sent_rows, :].astype(F32)
            swap_out[q] = value.astype(BF16)
            return carry

        lax.fori_loop(0, count, send_tile, 0)
        copy = remote(2 * stages, swap_out, swap_got, partner)

        def keep_tile(q, carry):
            cross_acc[q] = cross_keep[q, kept_rows, :].astype(F32) + cross_got0[
                q, kept_rows, :
            ].astype(F32)
            return carry

        lax.fori_loop(0, count, keep_tile, 0)
        return copy

    def cross_stage(t):
        size = sizes[t]

        def total(q):
            other = swap_got[q] if t == 0 else cross_got[starts[t] + q]
            return cross_acc[q] + other.astype(F32)

        if size == 1:
            cross_acc[0] = total(0)
            return None
        send_at = starts[t + 1]

        def send_tile(i, carry):
            cross_out[send_at + i] = total(size // 2 + i).astype(BF16)
            return carry

        lax.fori_loop(0, size // 2, send_tile, 0)
        copy = remote(
            stages + t + 1,
            cross_out.at[pl.ds(send_at, size // 2)],
            cross_got.at[pl.ds(send_at, size // 2)],
            peers[t + 1],
        )

        def keep_tile(q, carry):
            cross_acc[q] = total(q)
            return carry

        lax.fori_loop(0, size // 2, keep_tile, 0)
        return copy

    cross_copy = remote(stages, cross_send, cross_got0, peers[0])
    same_copy = remote(0, same_send, same_got.at[pl.ds(0, count)], peers[0])
    cross_copy.wait()
    swap_copy = cross_first()
    same_copy.wait()
    same_copy = same_stage(0)
    cross_copy = swap_copy
    for t in range(stages):
        if t + 1 < stages:
            same_copy.wait()
            same_copy = same_stage(t + 1)
        cross_copy.wait()
        cross_copy = cross_stage(t)
    last_out[...] = cross_acc[0].astype(BF16)
    copy = remote(2 * stages + 1, last_out, last_got, partner)

    value = same_acc[0]
    d = value[3 * NB :]
    below = value[NB : 2 * NB]
    diagonal = jnp.concatenate([d[0:1] + d[1:2], d[2:3] + d[3:4]], axis=1)
    same = jnp.concatenate(
        [
            jnp.concatenate([value[:NB], below.T], axis=1),
            jnp.concatenate([below, value[2 * NB : 3 * NB]], axis=1),
        ],
        axis=0,
    )
    eye = lax.broadcasted_iota(jnp.int32, (rows, rows), 0) == lax.broadcasted_iota(
        jnp.int32, (rows, rows), 1
    )
    same = jnp.where(eye, diagonal, same)
    full[kept_rows, :] = cross_acc[0]
    copy.wait()
    full[sent_rows, :] = last_got[...].astype(F32)

    @pl.when(half == 0)
    def _():
        out_ref[0, :, :rows] = target_ref[0, :, :rows] - same
        out_ref[0, :, rows:] = target_ref[0, :, rows:] - full[...]

    @pl.when(half == 1)
    def _():
        out_ref[0, :, :rows] = target_ref[0, :, :rows] - full[...].T
        out_ref[0, :, rows:] = target_ref[0, :, rows:] - same


def reduced(order, same_keep, same_send, cross_keep, cross_send, target_tiles):
    count, rows = cross_keep.shape[:2]
    tile = same_keep.shape[1:]
    part = (NB, rows)
    stages = len(order)
    vmem = pl.BlockSpec(memory_space=pltpu.VMEM)
    return pl.pallas_call(
        functools.partial(reduce_kernel, order),
        out_shape=jax.ShapeDtypeStruct(target_tiles.shape, F32),
        in_specs=[vmem] * 5,
        out_specs=vmem,
        scratch_shapes=[
            pltpu.VMEM((count,) + tile, F32),
            pltpu.VMEM((count,) + tile, BF16),
            pltpu.VMEM((2 * count,) + tile, BF16),
            pltpu.VMEM((count,) + part, F32),
            pltpu.VMEM((count,) + part, BF16),
            pltpu.VMEM((count, rows, rows), BF16),
            pltpu.VMEM((count,) + part, BF16),
            pltpu.VMEM((count,) + part, BF16),
            pltpu.VMEM((count,) + part, BF16),
            pltpu.VMEM(part, BF16),
            pltpu.VMEM(part, BF16),
            pltpu.VMEM((rows, rows), F32),
            pltpu.SemaphoreType.DMA((2 * stages + 2,)),
            pltpu.SemaphoreType.DMA((2 * stages + 2,)),
        ],
        compiler_params=pltpu.CompilerParams(
            collective_id=1, has_side_effects=True, vmem_limit_bytes=48 * 2**20
        ),
        name="reduce",
    )(same_keep, same_send, cross_keep, cross_send, target_tiles)


def gathered(slot, panel_blocks, hi, lo, columns):
    count, blocks, rows, width = panel_blocks.shape
    inverse = hi.astype(F32) + lo.astype(F32)
    solved = jnp.einsum("sjaw,swv->sjav", panel_blocks, inverse, precision=lax.Precision.HIGHEST)
    rounded = solved.astype(BF16)
    tiles = jnp.zeros((columns, rows, width), F32)
    for s in range(count):
        full = lax.all_gather(rounded[s], "row", axis=1, tiled=True)
        products = jnp.einsum("jaw,jbw->jab", rounded[s], full, preferred_element_type=F32)
        tiles = tiles.at[slot[s]].add(products)
    return solved, tiles


def on_device(columns, halves, diag_blocks, panel_blocks, ancestors, target_ids, target_tiles):
    me, half = lax.axis_index("col"), lax.axis_index("row")
    paired = halves == 2 and panel_blocks.shape[0] == 2 and panel_blocks.shape[2] == 2 * NB
    swap = [(0, 1), (1, 0)]
    if paired:
        outgoing = lax.dynamic_index_in_dim(panel_blocks, 1 - half, 0, keepdims=False).astype(BF16)
        other = lax.ppermute(outgoing, "row", swap)
    place = jnp.arange(columns, dtype=jnp.int32)
    if paired:
        near_ids = ids_by_distance(target_ids, columns)
        matches = ancestors[:, :, None] == near_ids[None, None, :]
        distance = jnp.sum(jnp.where(matches, place[None, None, :], 0), axis=2)
    else:
        all_ids = lax.all_gather(target_ids, "col", axis=0, tiled=True)
        matches = ancestors[:, :, None] == all_ids[None, None, :]
        position = jnp.sum(jnp.where(matches, place[None, None, :], 0), axis=2)
        distance = (position ^ me).astype(jnp.int32)
    bits = list(range(columns.bit_length() - 1))
    slot = jnp.zeros_like(distance)
    for bit in bits:
        slot = slot * 2 + ((distance >> bit) & 1)
    hi, lo = inverse_factors(diag_blocks)
    if not paired:
        panel_factor, tiles = gathered(slot, panel_blocks, hi, lo, columns)
        keep, send = tiles[: columns // 2], tiles[columns // 2 :].astype(BF16)
        return (panel_factor, target_tiles - halve_and_add(keep, send, bits, columns)[None])
    mine = half.astype(jnp.int32).reshape(1)
    panel_factor, same_keep, same_send, cross_keep, cross_send = panel_products(
        slot, mine, panel_blocks, other, hi, lo, columns
    )
    updated = reduced(bits, same_keep, same_send, cross_keep, cross_send, target_tiles)
    return (panel_factor, updated)


def solution(mesh):
    in_specs = (
        P("col", None, None),
        P("col", None, "row", None),
        P("col", None),
        P("col"),
        P("col", "row", None),
    )
    out_specs = (P("col", None, "row", None), P("col", "row", None))
    return jax.shard_map(
        functools.partial(on_device, mesh.shape["col"], mesh.shape["row"]),
        mesh=mesh,
        in_specs=in_specs,
        out_specs=out_specs,
        check_vma=False,
    )
```

```python
import functools

import jax
import jax.numpy as jnp
from jax import lax
from jax.experimental import pallas as pl
from jax.experimental.pallas import tpu as pltpu
from jax.sharding import PartitionSpec as P

NB = 128
F32 = jnp.float32
BF16 = jnp.bfloat16


def dot_exact(a, b):
    return jnp.dot(a, b, preferred_element_type=F32, precision=lax.Precision.HIGHEST)


def eliminate(blocks, frozen):
    count = len(blocks)
    lane = lax.broadcasted_iota(jnp.int32, (1, NB), 1)
    sub = lax.broadcasted_iota(jnp.int32, (8, NB), 0)
    head = [None] * count
    tail = list(blocks)
    for g in range(NB // 8):
        rows = NB - 8 * g - 8
        cols_head, cols_tail = [], []
        for s in range(count):
            a = tail[s]
            head[s], tail[s] = a[:8], (a[8:] if rows else None)
            cols_head.append(
                [jnp.broadcast_to(head[s][:, 8 * g + m : 8 * g + m + 1], (8, NB)) for m in range(8)]
            )
            cols_tail.append(
                [jnp.broadcast_to(tail[s][:, 8 * g + m : 8 * g + m + 1], (rows, NB)) for m in range(8)]
                if rows
                else None
            )
        for k in range(8):
            at = lane == 8 * g + k
            for s in range(count):
                ch, ct = cols_head[s], cols_tail[s]
                inv = lax.rsqrt(ch[k][k : k + 1, :])
                recip = inv * inv
                row = head[s][k : k + 1, :]
                frozen[s, 8 * g + k : 8 * g + k + 1, :] = jnp.where(at, inv, row * inv)
                step = jnp.where(at, 1.0 + recip, row * recip)
                below = jnp.where(sub > k, ch[k], 0.0)
                head[s] = head[s] - below * step
                if rows:
                    tail[s] = tail[s] - ct[k] * step
                for m in range(k + 1, 8):
                    scale = ch[m][k : k + 1, :] * recip
                    ch[m] = ch[m] - below * scale
                    if rows:
                        ct[m] = ct[m] - ct[k] * scale


def factor_kernel(diag_ref, hi_ref, lo_ref, work, frozen):
    count, width, _ = diag_ref.shape
    work[...] = diag_ref[...]
    lower = lax.broadcasted_iota(jnp.int32, (NB, NB), 0) >= lax.broadcasted_iota(
        jnp.int32, (NB, NB), 1
    )
    lane_block = lax.broadcasted_iota(jnp.int32, (1, width), 1) // NB

    def block_step(b, carry):
        here = pl.ds(pl.multiple_of(b * NB, NB), NB)
        eliminate([work[s, here, here] for s in range(count)], frozen)
        own = lane_block == b
        for s in range(count):
            inverse = jnp.where(lower, frozen[s], 0.0)
            work[s, here, :] = dot_exact(inverse, work[s, here, :])
            work[s, here, here] = inverse

        def trailing(i, carry):
            there = pl.ds(pl.multiple_of(i * NB, NB), NB)
            for s in range(count):
                left = work[s, here, there].T
                old = jnp.where(own, 0.0, work[s, there, :])
                work[s, there, :] = old - dot_exact(left, work[s, here, :])
            return carry

        return lax.fori_loop(b + 1, width // NB, trailing, carry)

    lax.fori_loop(0, width // NB, block_step, 0)
    keep = lax.broadcasted_iota(jnp.int32, (width, width), 0) >= lax.broadcasted_iota(
        jnp.int32, (width, width), 1
    )
    for s in range(count):
        inverse = jnp.where(keep, work[s], 0.0).T
        hi = inverse.astype(BF16)
        hi_ref[s] = hi
        lo_ref[s] = (inverse - hi.astype(F32)).astype(BF16)


def inverse_factors(diag_blocks):
    count, width, _ = diag_blocks.shape
    out = jax.ShapeDtypeStruct((count, width, width), BF16)
    return pl.pallas_call(
        factor_kernel,
        out_shape=(out, out),
        in_specs=[pl.BlockSpec(memory_space=pltpu.VMEM)],
        out_specs=(pl.BlockSpec(memory_space=pltpu.VMEM),) * 2,
        scratch_shapes=[
            pltpu.VMEM((count, width, width), F32),
            pltpu.VMEM((count, NB, NB), F32),
        ],
        compiler_params=pltpu.CompilerParams(vmem_limit_bytes=40 * 2**20),
        cost_estimate=pl.CostEstimate(
            flops=40 * 10**9, bytes_accessed=4 * count * width * width, transcendentals=0
        ),
        name="factor",
    )(diag_blocks)


def dot_nt(a, b):
    return lax.dot_general(a, b, (((1,), (1,)), ((), ())), preferred_element_type=F32)


def split_diagonal(tail, first, second, extra):
    rest = 0.0
    for at, term in ((0, first), (2, second)):
        total = tail[at : at + 1] + tail[at + 1 : at + 2] + term
        top = total.astype(BF16).astype(F32)
        rest = jnp.where(extra == at, top, jnp.where(extra == at + 1, total - top, rest))
    return rest


def place_tile(tile, slot, keep_ref, send_ref):
    half = keep_ref.shape[0]

    @pl.when(slot < half)
    def _():
        keep_ref[slot] = tile(keep_ref[slot])

    @pl.when(slot >= half)
    def _():
        send_ref[slot - half] = tile(send_ref[slot - half])


def panel_kernel(
    slot_ref, mine_ref, panel_ref, other_ref, hi_ref, lo_ref,
    out_ref, same_keep, same_send, cross_keep, cross_send,
):
    s, j = pl.program_id(0), pl.program_id(1)
    blocks, rows, width = panel_ref.shape[1:]
    low = width // 2

    @pl.when((s == 0) & (j == 0))
    def _():
        for ref in (same_keep, same_send, cross_keep, cross_send):
            ref[...] = jnp.zeros_like(ref)

    def times_inverse(*pairs):
        left = jnp.dot(
            jnp.concatenate([lhs[:, :low] for lhs, _ in pairs], axis=1),
            jnp.concatenate([factor[:low, :low] for _, factor in pairs], axis=0),
            preferred_element_type=F32,
        )
        right = jnp.dot(
            jnp.concatenate([lhs for lhs, _ in pairs], axis=1),
            jnp.concatenate([factor[:, low:] for _, factor in pairs], axis=0),
            preferred_element_type=F32,
        )
        return jnp.concatenate([left, right], axis=1)

    hi, lo = hi_ref[0], lo_ref[0]
    rhs = panel_ref[0].reshape(blocks * rows, width)
    rhs_hi = rhs.astype(BF16)
    rhs_lo = (rhs - rhs_hi.astype(F32)).astype(BF16)
    solved = times_inverse((rhs_hi, hi), (rhs_lo, hi), (rhs_hi, lo))
    out_ref[0] = solved.reshape(blocks, rows, width)
    rounded = solved.astype(BF16).reshape(blocks, rows, width)
    diagonal = lax.broadcasted_iota(jnp.int32, (rows, rows), 0) == lax.broadcasted_iota(
        jnp.int32, (rows, rows), 1
    )
    extra = lax.broadcasted_iota(jnp.int32, (16, NB), 0)
    for i in range(blocks):
        product = dot_nt(rounded[i], rounded[i])
        sums = jnp.sum(jnp.where(diagonal, product, 0.0), axis=0, keepdims=True)
        product = jnp.where(diagonal, 0.0, product)
        lower = [product[:NB, :NB], product[NB:, :NB], product[NB:, NB:]]

        def added(old):
            rest = split_diagonal(old[3 * NB :].astype(F32), sums[:, :NB], sums[:, NB:], extra)
            return jnp.concatenate(
                [old[: 3 * NB].astype(F32) + jnp.concatenate(lower, axis=0), rest], axis=0
            ).astype(BF16)

        place_tile(added, slot_ref[s, j * blocks + i], same_keep, same_send)

    @pl.when(s == mine_ref[0])
    def _():
        got = other_ref[...].reshape(blocks * rows, width)
        partner = times_inverse((got, hi), (got, lo)).astype(BF16)
        partner = partner.reshape(blocks, rows, width)
        for i in range(blocks):
            slot = slot_ref[s, j * blocks + i]
            first, second = rounded[i], partner[i]

            @pl.when(mine_ref[0] == 0)
            def _():
                product = dot_nt(first, second).astype(BF16)
                place_tile(lambda old: product, slot, cross_keep, cross_send)

            @pl.when(mine_ref[0] != 0)
            def _():
                product = dot_nt(second, first).astype(BF16)
                place_tile(lambda old: product, slot, cross_keep, cross_send)


def panel_products(slot, mine, panel_blocks, other, hi, lo, targets):
    count, blocks, rows, width = panel_blocks.shape
    step = 2 if blocks % 2 == 0 else 1
    steps = blocks // step
    shapes = [(targets // 2, 3 * NB + 16, NB)] * 2 + [(targets // 2, rows, rows)] * 2
    whole = [pl.BlockSpec(shape, lambda s, j, slot, mine: (0, 0, 0)) for shape in shapes]
    factor = pl.BlockSpec((1, width, width), lambda s, j, slot, mine: (s, 0, 0))
    panel = pl.BlockSpec((1, step, rows, width), lambda s, j, slot, mine: (s, j, 0, 0))

    def other_at(s, j, slot, mine):
        return (jnp.where(s == mine[0], j, jnp.where(s < mine[0], 0, steps - 1)), 0, 0)

    return pl.pallas_call(
        panel_kernel,
        out_shape=[jax.ShapeDtypeStruct(panel_blocks.shape, F32)]
        + [jax.ShapeDtypeStruct(shape, BF16) for shape in shapes],
        grid_spec=pltpu.PrefetchScalarGridSpec(
            num_scalar_prefetch=2,
            grid=(count, steps),
            in_specs=[panel, pl.BlockSpec((step, rows, width), other_at), factor, factor],
            out_specs=[panel] + whole,
        ),
        compiler_params=pltpu.CompilerParams(
            vmem_limit_bytes=56 * 2**20, dimension_semantics=("arbitrary", "arbitrary")
        ),
        name="panel",
    )(slot, mine, panel_blocks, other, hi, lo)


def halve_and_add(keep, send, order, columns):
    shape = keep.shape[1:]
    for bit in order:
        got = lax.ppermute(send, "col", [(c, c ^ (1 << bit)) for c in range(columns)])
        value = keep.astype(F32) + got.astype(F32)
        half = value.shape[0] // 2
        if half:
            keep, send = value[:half], value[half:].astype(BF16)
    return value.reshape(shape)


def flipped(index, bits):
    bit = 1
    other = index
    while bit <= bits:
        if bits & bit:
            other = other + bit * (1 - 2 * ((index // bit) % 2))
        bit *= 2
    return other


def meet(peers):
    barrier = pltpu.get_barrier_semaphore()
    for peer in peers:
        pl.semaphore_signal(barrier, inc=1, device_id=peer, device_id_type=pl.DeviceIdType.MESH)
    pl.semaphore_wait(barrier, len(peers))


def ids_kernel(own_ref, out_ref, landed, send_sem, recv_sem):
    columns = out_ref.shape[0]
    me, half = lax.axis_index("col"), lax.axis_index("row")
    peers = [(flipped(me, q), half) for q in range(1, columns)]
    meet(peers)
    copies = []
    for q in range(1, columns):
        copy = pltpu.make_async_remote_copy(
            src_ref=own_ref,
            dst_ref=landed.at[q],
            send_sem=send_sem.at[q],
            recv_sem=recv_sem.at[q],
            device_id=peers[q - 1],
            device_id_type=pl.DeviceIdType.MESH,
        )
        copy.start()
        copies.append(copy)
    out_ref[0] = own_ref[...]
    for q, copy in enumerate(copies, 1):
        copy.wait()
        out_ref[q] = landed[q]


def ids_by_distance(target_ids, columns):
    own = jnp.broadcast_to(target_ids, (8, 128))
    out = pl.pallas_call(
        ids_kernel,
        out_shape=jax.ShapeDtypeStruct((columns, 8, 128), jnp.int32),
        in_specs=[pl.BlockSpec(memory_space=pltpu.VMEM)],
        out_specs=pl.BlockSpec(memory_space=pltpu.VMEM),
        scratch_shapes=[
            pltpu.VMEM((columns, 8, 128), jnp.int32),
            pltpu.SemaphoreType.DMA((columns,)),
            pltpu.SemaphoreType.DMA((columns,)),
        ],
        compiler_params=pltpu.CompilerParams(collective_id=0, has_side_effects=True),
        name="ids",
    )(own)
    return out[:, 0, 0]


def reduce_kernel(
    order, same_held, same_send, cross_held, cross_send, target_ref, out_ref,
    same_keep, cross_keep, local_sem,
    same_acc, same_out, same_got, cross_acc, cross_out, cross_got0, cross_got,
    swap_out, swap_got, last_out, last_got, full, send_sem, recv_sem,
):
    me, half = lax.axis_index("col"), lax.axis_index("row")
    partner = (me, 1 - half)
    peers = [(flipped(me, 1 << bit), half) for bit in order]
    stages = len(order)
    rows = 2 * NB
    cross_load = pltpu.make_async_copy(cross_held, cross_keep, local_sem.at[0])
    same_load = pltpu.make_async_copy(same_held, same_keep, local_sem.at[1])
    cross_load.start()
    same_load.start()
    meet(peers + [partner])
    extra = lax.broadcasted_iota(jnp.int32, (16, NB), 0)
    kept_rows = pl.ds(pl.multiple_of(half * NB, NB), NB)
    sent_rows = pl.ds(pl.multiple_of((1 - half) * NB, NB), NB)
    count = same_keep.shape[0]
    sizes = [count >> t for t in range(stages)]
    starts = [sum(sizes[1:t]) for t in range(stages)]

    def remote(number, src, dst, device):
        copy = pltpu.make_async_remote_copy(
            src_ref=src,
            dst_ref=dst,
            send_sem=send_sem.at[number],
            recv_sem=recv_sem.at[number],
            device_id=device,
            device_id_type=pl.DeviceIdType.MESH,
        )
        copy.start()
        return copy

    def same_stage(t):
        size = sizes[t]
        base = 0 if t == 0 else count + starts[t]

        def total(q):
            mine = same_keep[q].astype(F32) if t == 0 else same_acc[q]
            return mine + same_got[base + q].astype(F32)

        if size == 1:
            same_acc[0] = total(0)
            return None
        send_at = starts[t + 1]

        def send_tile(i, carry):
            value = total(size // 2 + i)
            rest = split_diagonal(value[3 * NB :], 0.0, 0.0, extra)
            same_out[send_at + i] = jnp.concatenate([value[: 3 * NB], rest], axis=0).astype(BF16)
            return carry

        lax.fori_loop(0, size // 2, send_tile, 0)
        copy = remote(
            t + 1,
            same_out.at[pl.ds(send_at, size // 2)],
            same_got.at[pl.ds(count + send_at, size // 2)],
            peers[t + 1],
        )

        def keep_tile(q, carry):
            same_acc[q] = total(q)
            return carry

        lax.fori_loop(0, size // 2, keep_tile, 0)
        return copy

    def cross_first():
        def send_tile(q, carry):
            value = cross_keep[q, sent_rows, :].astype(F32) + cross_got0[q, sent_rows, :].astype(F32)
            swap_out[q] = value.astype(BF16)
            return carry

        lax.fori_loop(0, count, send_tile, 0)
        copy = remote(2 * stages, swap_out, swap_got, partner)

        def keep_tile(q, carry):
            cross_acc[q] = cross_keep[q, kept_rows, :].astype(F32) + cross_got0[
                q, kept_rows, :
            ].astype(F32)
            return carry

        lax.fori_loop(0, count, keep_tile, 0)
        return copy

    def cross_stage(t):
        size = sizes[t]

        def total(q):
            other = swap_got[q] if t == 0 else cross_got[starts[t] + q]
            return cross_acc[q] + other.astype(F32)

        if size == 1:
            cross_acc[0] = total(0)
            return None
        send_at = starts[t + 1]

        def send_tile(i, carry):
            cross_out[send_at + i] = total(size // 2 + i).astype(BF16)
            return carry

        lax.fori_loop(0, size // 2, send_tile, 0)
        copy = remote(
            stages + t + 1,
            cross_out.at[pl.ds(send_at, size // 2)],
            cross_got.at[pl.ds(send_at, size // 2)],
            peers[t + 1],
        )

        def keep_tile(q, carry):
            cross_acc[q] = total(q)
            return carry

        lax.fori_loop(0, size // 2, keep_tile, 0)
        return copy

    cross_copy = remote(stages, cross_send, cross_got0, peers[0])
    same_copy = remote(0, same_send, same_got.at[pl.ds(0, count)], peers[0])
    cross_load.wait()
    cross_copy.wait()
    swap_copy = cross_first()
    same_load.wait()
    same_copy.wait()
    same_copy = same_stage(0)
    cross_copy = swap_copy
    for t in range(stages):
        if t + 1 < stages:
            same_copy.wait()
            same_copy = same_stage(t + 1)
        cross_copy.wait()
        cross_copy = cross_stage(t)
    last_out[...] = cross_acc[0].astype(BF16)
    copy = remote(2 * stages + 1, last_out, last_got, partner)

    value = same_acc[0]
    d = value[3 * NB :]
    below = value[NB : 2 * NB]
    diagonal = jnp.concatenate([d[0:1] + d[1:2], d[2:3] + d[3:4]], axis=1)
    same = jnp.concatenate(
        [
            jnp.concatenate([value[:NB], below.T], axis=1),
            jnp.concatenate([below, value[2 * NB : 3 * NB]], axis=1),
        ],
        axis=0,
    )
    eye = lax.broadcasted_iota(jnp.int32, (rows, rows), 0) == lax.broadcasted_iota(
        jnp.int32, (rows, rows), 1
    )
    same = jnp.where(eye, diagonal, same)
    full[kept_rows, :] = cross_acc[0]
    copy.wait()
    full[sent_rows, :] = last_got[...].astype(F32)

    @pl.when(half == 0)
    def _():
        out_ref[0, :, :rows] = target_ref[0, :, :rows] - same
        out_ref[0, :, rows:] = target_ref[0, :, rows:] - full[...]

    @pl.when(half == 1)
    def _():
        out_ref[0, :, :rows] = target_ref[0, :, :rows] - full[...].T
        out_ref[0, :, rows:] = target_ref[0, :, rows:] - same


def reduced(order, same_keep, same_send, cross_keep, cross_send, target_tiles):
    count, rows = cross_keep.shape[:2]
    tile = same_keep.shape[1:]
    part = (NB, rows)
    stages = len(order)
    vmem = pl.BlockSpec(memory_space=pltpu.VMEM)
    return pl.pallas_call(
        functools.partial(reduce_kernel, order),
        out_shape=jax.ShapeDtypeStruct(target_tiles.shape, F32),
        in_specs=[pl.BlockSpec(memory_space=pl.ANY)] * 4 + [vmem],
        out_specs=vmem,
        scratch_shapes=[
            pltpu.VMEM(same_keep.shape, BF16),
            pltpu.VMEM(cross_keep.shape, BF16),
            pltpu.SemaphoreType.DMA((2,)),
            pltpu.VMEM((count,) + tile, F32),
            pltpu.VMEM((count,) + tile, BF16),
            pltpu.VMEM((2 * count,) + tile, BF16),
            pltpu.VMEM((count,) + part, F32),
            pltpu.VMEM((count,) + part, BF16),
            pltpu.VMEM((count, rows, rows), BF16),
            pltpu.VMEM((count,) + part, BF16),
            pltpu.VMEM((count,) + part, BF16),
            pltpu.VMEM((count,) + part, BF16),
            pltpu.VMEM(part, BF16),
            pltpu.VMEM(part, BF16),
            pltpu.VMEM((rows, rows), F32),
            pltpu.SemaphoreType.DMA((2 * stages + 2,)),
            pltpu.SemaphoreType.DMA((2 * stages + 2,)),
        ],
        compiler_params=pltpu.CompilerParams(
            collective_id=1, has_side_effects=True, vmem_limit_bytes=48 * 2**20
        ),
        name="reduce",
    )(same_keep, same_send, cross_keep, cross_send, target_tiles)


def gathered(slot, panel_blocks, hi, lo, columns):
    count, blocks, rows, width = panel_blocks.shape
    inverse = hi.astype(F32) + lo.astype(F32)
    solved = jnp.einsum("sjaw,swv->sjav", panel_blocks, inverse, precision=lax.Precision.HIGHEST)
    rounded = solved.astype(BF16)
    tiles = jnp.zeros((columns, rows, width), F32)
    for s in range(count):
        full = lax.all_gather(rounded[s], "row", axis=1, tiled=True)
        products = jnp.einsum("jaw,jbw->jab", rounded[s], full, preferred_element_type=F32)
        tiles = tiles.at[slot[s]].add(products)
    return solved, tiles


def on_device(columns, halves, diag_blocks, panel_blocks, ancestors, target_ids, target_tiles):
    me, half = lax.axis_index("col"), lax.axis_index("row")
    paired = halves == 2 and panel_blocks.shape[0] == 2 and panel_blocks.shape[2] == 2 * NB
    swap = [(0, 1), (1, 0)]
    if paired:
        outgoing = lax.dynamic_index_in_dim(panel_blocks, 1 - half, 0, keepdims=False).astype(BF16)
        other = lax.ppermute(outgoing, "row", swap)
    place = jnp.arange(columns, dtype=jnp.int32)
    if paired:
        near_ids = ids_by_distance(target_ids, columns)
        matches = ancestors[:, :, None] == near_ids[None, None, :]
        distance = jnp.sum(jnp.where(matches, place[None, None, :], 0), axis=2)
    else:
        all_ids = lax.all_gather(target_ids, "col", axis=0, tiled=True)
        matches = ancestors[:, :, None] == all_ids[None, None, :]
        position = jnp.sum(jnp.where(matches, place[None, None, :], 0), axis=2)
        distance = (position ^ me).astype(jnp.int32)
    bits = list(range(columns.bit_length() - 1))
    slot = jnp.zeros_like(distance)
    for bit in bits:
        slot = slot * 2 + ((distance >> bit) & 1)
    hi, lo = inverse_factors(diag_blocks)
    if not paired:
        panel_factor, tiles = gathered(slot, panel_blocks, hi, lo, columns)
        keep, send = tiles[: columns // 2], tiles[columns // 2 :].astype(BF16)
        return (panel_factor, target_tiles - halve_and_add(keep, send, bits, columns)[None])
    mine = half.astype(jnp.int32).reshape(1)
    panel_factor, same_keep, same_send, cross_keep, cross_send = panel_products(
        slot, mine, panel_blocks, other, hi, lo, columns
    )
    updated = reduced(bits, same_keep, same_send, cross_keep, cross_send, target_tiles)
    return (panel_factor, updated)


def solution(mesh):
    in_specs = (
        P("col", None, None),
        P("col", None, "row", None),
        P("col", None),
        P("col"),
        P("col", "row", None),
    )
    out_specs = (P("col", None, "row", None), P("col", "row", None))
    return jax.shard_map(
        functools.partial(on_device, mesh.shape["col"], mesh.shape["row"]),
        mesh=mesh,
        in_specs=in_specs,
        out_specs=out_specs,
        check_vma=False,
    )
```

```python
import functools

import jax
import jax.numpy as jnp
from jax import lax
from jax.experimental import pallas as pl
from jax.experimental.pallas import tpu as pltpu
from jax.sharding import PartitionSpec as P

NB = 128
F32 = jnp.float32
BF16 = jnp.bfloat16


def dot_exact(a, b):
    return jnp.dot(a, b, preferred_element_type=F32, precision=lax.Precision.HIGHEST)


def eliminate(blocks, frozen):
    count = len(blocks)
    lane = lax.broadcasted_iota(jnp.int32, (1, NB), 1)
    sub = lax.broadcasted_iota(jnp.int32, (8, NB), 0)
    head = [None] * count
    tail = list(blocks)
    for g in range(NB // 8):
        rows = NB - 8 * g - 8
        cols_head, cols_tail = [], []
        for s in range(count):
            a = tail[s]
            head[s], tail[s] = a[:8], (a[8:] if rows else None)
            cols_head.append(
                [jnp.broadcast_to(head[s][:, 8 * g + m : 8 * g + m + 1], (8, NB)) for m in range(8)]
            )
            cols_tail.append(
                [jnp.broadcast_to(tail[s][:, 8 * g + m : 8 * g + m + 1], (rows, NB)) for m in range(8)]
                if rows
                else None
            )
        for k in range(8):
            at = lane == 8 * g + k
            for s in range(count):
                ch, ct = cols_head[s], cols_tail[s]
                inv = lax.rsqrt(ch[k][k : k + 1, :])
                recip = inv * inv
                row = head[s][k : k + 1, :]
                frozen[s, 8 * g + k : 8 * g + k + 1, :] = jnp.where(at, inv, row * inv)
                step = jnp.where(at, 1.0 + recip, row * recip)
                below = jnp.where(sub > k, ch[k], 0.0)
                head[s] = head[s] - below * step
                if rows:
                    tail[s] = tail[s] - ct[k] * step
                for m in range(k + 1, 8):
                    scale = ch[m][k : k + 1, :] * recip
                    ch[m] = ch[m] - below * scale
                    if rows:
                        ct[m] = ct[m] - ct[k] * scale


def factor_kernel(diag_ref, hi_ref, lo_ref, work, frozen):
    count, width, _ = diag_ref.shape
    work[...] = diag_ref[...]
    lower = lax.broadcasted_iota(jnp.int32, (NB, NB), 0) >= lax.broadcasted_iota(
        jnp.int32, (NB, NB), 1
    )
    lane_block = lax.broadcasted_iota(jnp.int32, (1, width), 1) // NB

    def block_step(b, carry):
        here = pl.ds(pl.multiple_of(b * NB, NB), NB)
        eliminate([work[s, here, here] for s in range(count)], frozen)
        own = lane_block == b
        for s in range(count):
            inverse = jnp.where(lower, frozen[s], 0.0)
            work[s, here, :] = dot_exact(inverse, work[s, here, :])
            work[s, here, here] = inverse

        def trailing(i, carry):
            there = pl.ds(pl.multiple_of(i * NB, NB), NB)
            for s in range(count):
                left = work[s, here, there].T
                old = jnp.where(own, 0.0, work[s, there, :])
                work[s, there, :] = old - dot_exact(left, work[s, here, :])
            return carry

        return lax.fori_loop(b + 1, width // NB, trailing, carry)

    lax.fori_loop(0, width // NB, block_step, 0)
    keep = lax.broadcasted_iota(jnp.int32, (width, width), 0) >= lax.broadcasted_iota(
        jnp.int32, (width, width), 1
    )
    for s in range(count):
        inverse = jnp.where(keep, work[s], 0.0).T
        hi = inverse.astype(BF16)
        hi_ref[s] = hi
        lo_ref[s] = (inverse - hi.astype(F32)).astype(BF16)


def inverse_factors(diag_blocks):
    count, width, _ = diag_blocks.shape
    out = jax.ShapeDtypeStruct((count, width, width), BF16)
    return pl.pallas_call(
        factor_kernel,
        out_shape=(out, out),
        in_specs=[pl.BlockSpec(memory_space=pltpu.VMEM)],
        out_specs=(pl.BlockSpec(memory_space=pltpu.VMEM),) * 2,
        scratch_shapes=[
            pltpu.VMEM((count, width, width), F32),
            pltpu.VMEM((count, NB, NB), F32),
        ],
        compiler_params=pltpu.CompilerParams(vmem_limit_bytes=40 * 2**20),
        cost_estimate=pl.CostEstimate(
            flops=40 * 10**9, bytes_accessed=4 * count * width * width, transcendentals=0
        ),
        name="factor",
    )(diag_blocks)


def dot_nt(a, b):
    return lax.dot_general(a, b, (((1,), (1,)), ((), ())), preferred_element_type=F32)


def split_diagonal(tail, first, second, extra):
    rest = 0.0
    for at, term in ((0, first), (2, second)):
        total = tail[at : at + 1] + tail[at + 1 : at + 2] + term
        top = total.astype(BF16).astype(F32)
        rest = jnp.where(extra == at, top, jnp.where(extra == at + 1, total - top, rest))
    return rest


def place_tile(tile, slot, keep_ref, send_ref):
    half = keep_ref.shape[0]

    @pl.when(slot < half)
    def _():
        keep_ref[slot] = tile(keep_ref[slot])

    @pl.when(slot >= half)
    def _():
        send_ref[slot - half] = tile(send_ref[slot - half])


def panel_kernel(
    slot_ref, mine_ref, panel_ref, other_ref, hi_ref, lo_ref,
    out_ref, same_keep, same_send, cross_keep, cross_send,
):
    s, j = pl.program_id(0), pl.program_id(1)
    blocks, rows, width = panel_ref.shape[1:]
    low = width // 2

    @pl.when((s == 0) & (j == 0))
    def _():
        for ref in (same_keep, same_send, cross_keep, cross_send):
            ref[...] = jnp.zeros_like(ref)

    def times_inverse(*pairs):
        left = jnp.dot(
            jnp.concatenate([lhs[:, :low] for lhs, _ in pairs], axis=1),
            jnp.concatenate([factor[:low, :low] for _, factor in pairs], axis=0),
            preferred_element_type=F32,
        )
        right = jnp.dot(
            jnp.concatenate([lhs for lhs, _ in pairs], axis=1),
            jnp.concatenate([factor[:, low:] for _, factor in pairs], axis=0),
            preferred_element_type=F32,
        )
        return jnp.concatenate([left, right], axis=1)

    hi, lo = hi_ref[0], lo_ref[0]
    rhs = panel_ref[0].reshape(blocks * rows, width)
    rhs_hi = rhs.astype(BF16)
    rhs_lo = (rhs - rhs_hi.astype(F32)).astype(BF16)
    solved = times_inverse((rhs_hi, hi), (rhs_lo, hi), (rhs_hi, lo))
    out_ref[0] = solved.reshape(blocks, rows, width)
    rounded = solved.astype(BF16).reshape(blocks, rows, width)
    diagonal = lax.broadcasted_iota(jnp.int32, (rows, rows), 0) == lax.broadcasted_iota(
        jnp.int32, (rows, rows), 1
    )
    extra = lax.broadcasted_iota(jnp.int32, (16, NB), 0)
    for i in range(blocks):
        product = dot_nt(rounded[i], rounded[i])
        sums = jnp.sum(jnp.where(diagonal, product, 0.0), axis=0, keepdims=True)
        product = jnp.where(diagonal, 0.0, product)
        lower = [product[:NB, :NB], product[NB:, :NB], product[NB:, NB:]]

        def added(old):
            rest = split_diagonal(old[3 * NB :].astype(F32), sums[:, :NB], sums[:, NB:], extra)
            return jnp.concatenate(
                [old[: 3 * NB].astype(F32) + jnp.concatenate(lower, axis=0), rest], axis=0
            ).astype(BF16)

        place_tile(added, slot_ref[s, j * blocks + i], same_keep, same_send)

    @pl.when(s == mine_ref[0])
    def _():
        got = other_ref[...].reshape(blocks * rows, width)
        partner = times_inverse((got, hi), (got, lo)).astype(BF16)
        partner = partner.reshape(blocks, rows, width)
        for i in range(blocks):
            slot = slot_ref[s, j * blocks + i]
            first, second = rounded[i], partner[i]

            @pl.when(mine_ref[0] == 0)
            def _():
                product = dot_nt(first, second).astype(BF16)
                place_tile(lambda old: product, slot, cross_keep, cross_send)

            @pl.when(mine_ref[0] != 0)
            def _():
                product = dot_nt(second, first).astype(BF16)
                place_tile(lambda old: product, slot, cross_keep, cross_send)


def panel_products(slot, mine, panel_blocks, other, hi, lo, targets):
    count, blocks, rows, width = panel_blocks.shape
    step = 2 if blocks % 2 == 0 else 1
    steps = blocks // step
    shapes = [(targets // 2, 3 * NB + 16, NB)] * 2 + [(targets // 2, rows, rows)] * 2
    whole = [pl.BlockSpec(shape, lambda s, j, slot, mine: (0, 0, 0)) for shape in shapes]
    factor = pl.BlockSpec((1, width, width), lambda s, j, slot, mine: (s, 0, 0))
    panel = pl.BlockSpec((1, step, rows, width), lambda s, j, slot, mine: (s, j, 0, 0))

    def other_at(s, j, slot, mine):
        return (jnp.where(s == mine[0], j, jnp.where(s < mine[0], 0, steps - 1)), 0, 0)

    return pl.pallas_call(
        panel_kernel,
        out_shape=[jax.ShapeDtypeStruct(panel_blocks.shape, F32)]
        + [jax.ShapeDtypeStruct(shape, BF16) for shape in shapes],
        grid_spec=pltpu.PrefetchScalarGridSpec(
            num_scalar_prefetch=2,
            grid=(count, steps),
            in_specs=[panel, pl.BlockSpec((step, rows, width), other_at), factor, factor],
            out_specs=[panel] + whole,
        ),
        compiler_params=pltpu.CompilerParams(
            vmem_limit_bytes=56 * 2**20, dimension_semantics=("arbitrary", "arbitrary")
        ),
        name="panel",
    )(slot, mine, panel_blocks, other, hi, lo)


def halve_and_add(keep, send, order, columns):
    shape = keep.shape[1:]
    for bit in order:
        got = lax.ppermute(send, "col", [(c, c ^ (1 << bit)) for c in range(columns)])
        value = keep.astype(F32) + got.astype(F32)
        half = value.shape[0] // 2
        if half:
            keep, send = value[:half], value[half:].astype(BF16)
    return value.reshape(shape)


def flipped(index, bits):
    bit = 1
    other = index
    while bit <= bits:
        if bits & bit:
            other = other + bit * (1 - 2 * ((index // bit) % 2))
        bit *= 2
    return other


def meet(peers):
    barrier = pltpu.get_barrier_semaphore()
    for peer in peers:
        pl.semaphore_signal(barrier, inc=1, device_id=peer, device_id_type=pl.DeviceIdType.MESH)
    pl.semaphore_wait(barrier, len(peers))


def ids_kernel(own_ref, out_ref, landed, send_sem, recv_sem):
    columns = out_ref.shape[0]
    me, half = lax.axis_index("col"), lax.axis_index("row")
    peers = [(flipped(me, q), half) for q in range(1, columns)]
    meet(peers)
    copies = []
    for q in range(1, columns):
        copy = pltpu.make_async_remote_copy(
            src_ref=own_ref,
            dst_ref=landed.at[q],
            send_sem=send_sem.at[q],
            recv_sem=recv_sem.at[q],
            device_id=peers[q - 1],
            device_id_type=pl.DeviceIdType.MESH,
        )
        copy.start()
        copies.append(copy)
    out_ref[0] = own_ref[...]
    for q, copy in enumerate(copies, 1):
        copy.wait()
        out_ref[q] = landed[q]


def ids_by_distance(target_ids, columns):
    own = jnp.broadcast_to(target_ids, (8, 128))
    out = pl.pallas_call(
        ids_kernel,
        out_shape=jax.ShapeDtypeStruct((columns, 8, 128), jnp.int32),
        in_specs=[pl.BlockSpec(memory_space=pltpu.VMEM)],
        out_specs=pl.BlockSpec(memory_space=pltpu.VMEM),
        scratch_shapes=[
            pltpu.VMEM((columns, 8, 128), jnp.int32),
            pltpu.SemaphoreType.DMA((columns,)),
            pltpu.SemaphoreType.DMA((columns,)),
        ],
        compiler_params=pltpu.CompilerParams(collective_id=0, has_side_effects=True),
        name="ids",
    )(own)
    return out[:, 0, 0]


def reduce_kernel(
    order, same_held, same_send, cross_held, cross_send, target_ref, out_ref,
    same_keep, cross_keep, local_sem,
    same_acc, same_out, same_got, cross_acc, cross_out, cross_got0, cross_got,
    swap_out, swap_got, last_out, last_got, full, send_sem, recv_sem,
):
    me, half = lax.axis_index("col"), lax.axis_index("row")
    partner = (me, 1 - half)
    peers = [(flipped(me, 1 << bit), half) for bit in order]
    stages = len(order)
    rows = 2 * NB
    cross_load = pltpu.make_async_copy(cross_held, cross_keep, local_sem.at[0])
    same_load = pltpu.make_async_copy(same_held, same_keep, local_sem.at[1])
    cross_load.start()
    same_load.start()
    meet(peers + [partner])
    extra = lax.broadcasted_iota(jnp.int32, (16, NB), 0)
    kept_rows = pl.ds(pl.multiple_of(half * NB, NB), NB)
    sent_rows = pl.ds(pl.multiple_of((1 - half) * NB, NB), NB)
    count = same_keep.shape[0]
    sizes = [count >> t for t in range(stages)]
    starts = [sum(sizes[1:t]) for t in range(stages)]

    def remote(number, src, dst, device):
        copy = pltpu.make_async_remote_copy(
            src_ref=src,
            dst_ref=dst,
            send_sem=send_sem.at[number],
            recv_sem=recv_sem.at[number],
            device_id=device,
            device_id_type=pl.DeviceIdType.MESH,
        )
        copy.start()
        return copy

    def same_stage(t):
        size = sizes[t]
        base = 0 if t == 0 else count + starts[t]

        def total(q):
            mine = same_keep[q].astype(F32) if t == 0 else same_acc[q]
            return mine + same_got[base + q].astype(F32)

        if size == 1:
            same_acc[0] = total(0)
            return None
        send_at = starts[t + 1]

        def send_tile(i, carry):
            value = total(size // 2 + i)
            rest = split_diagonal(value[3 * NB :], 0.0, 0.0, extra)
            same_out[send_at + i] = jnp.concatenate([value[: 3 * NB], rest], axis=0).astype(BF16)
            return carry

        lax.fori_loop(0, size // 2, send_tile, 0)
        copy = remote(
            t + 1,
            same_out.at[pl.ds(send_at, size // 2)],
            same_got.at[pl.ds(count + send_at, size // 2)],
            peers[t + 1],
        )

        def keep_tile(q, carry):
            same_acc[q] = total(q)
            return carry

        lax.fori_loop(0, size // 2, keep_tile, 0)
        return copy

    def cross_first():
        def send_tile(q, carry):
            value = cross_keep[q, sent_rows, :].astype(F32) + cross_got0[q, sent_rows, :].astype(F32)
            swap_out[q] = value.astype(BF16)
            return carry

        lax.fori_loop(0, count, send_tile, 0)
        copy = remote(2 * stages, swap_out, swap_got, partner)

        def keep_tile(q, carry):
            cross_acc[q] = cross_keep[q, kept_rows, :].astype(F32) + cross_got0[
                q, kept_rows, :
            ].astype(F32)
            return carry

        lax.fori_loop(0, count, keep_tile, 0)
        return copy

    def cross_stage(t):
        size = sizes[t]

        def total(q):
            other = swap_got[q] if t == 0 else cross_got[starts[t] + q]
            return cross_acc[q] + other.astype(F32)

        if size == 1:
            cross_acc[0] = total(0)
            return None
        send_at = starts[t + 1]

        def send_tile(i, carry):
            cross_out[send_at + i] = total(size // 2 + i).astype(BF16)
            return carry

        lax.fori_loop(0, size // 2, send_tile, 0)
        copy = remote(
            stages + t + 1,
            cross_out.at[pl.ds(send_at, size // 2)],
            cross_got.at[pl.ds(send_at, size // 2)],
            peers[t + 1],
        )

        def keep_tile(q, carry):
            cross_acc[q] = total(q)
            return carry

        lax.fori_loop(0, size // 2, keep_tile, 0)
        return copy

    cross_copy = remote(stages, cross_send, cross_got0, peers[0])
    same_copy = remote(0, same_send, same_got.at[pl.ds(0, count)], peers[0])
    cross_load.wait()
    cross_copy.wait()
    swap_copy = cross_first()
    same_load.wait()
    same_copy.wait()
    same_copy = same_stage(0)
    cross_copy = swap_copy
    for t in range(stages):
        if t + 1 < stages:
            same_copy.wait()
            same_copy = same_stage(t + 1)
        cross_copy.wait()
        cross_copy = cross_stage(t)
    last_out[...] = cross_acc[0].astype(BF16)
    copy = remote(2 * stages + 1, last_out, last_got, partner)

    value = same_acc[0]
    d = value[3 * NB :]
    below = value[NB : 2 * NB]
    diagonal = jnp.concatenate([d[0:1] + d[1:2], d[2:3] + d[3:4]], axis=1)
    same = jnp.concatenate(
        [
            jnp.concatenate([value[:NB], below.T], axis=1),
            jnp.concatenate([below, value[2 * NB : 3 * NB]], axis=1),
        ],
        axis=0,
    )
    eye = lax.broadcasted_iota(jnp.int32, (rows, rows), 0) == lax.broadcasted_iota(
        jnp.int32, (rows, rows), 1
    )
    same = jnp.where(eye, diagonal, same)
    full[kept_rows, :] = cross_acc[0]
    copy.wait()
    full[sent_rows, :] = last_got[...].astype(F32)

    @pl.when(half == 0)
    def _():
        out_ref[0, :, :rows] = target_ref[0, :, :rows] - same
        out_ref[0, :, rows:] = target_ref[0, :, rows:] - full[...]

    @pl.when(half == 1)
    def _():
        out_ref[0, :, :rows] = target_ref[0, :, :rows] - full[...].T
        out_ref[0, :, rows:] = target_ref[0, :, rows:] - same


def reduced(order, same_keep, same_send, cross_keep, cross_send, target_tiles):
    count, rows = cross_keep.shape[:2]
    tile = same_keep.shape[1:]
    part = (NB, rows)
    stages = len(order)
    vmem = pl.BlockSpec(memory_space=pltpu.VMEM)
    return pl.pallas_call(
        functools.partial(reduce_kernel, order),
        out_shape=jax.ShapeDtypeStruct(target_tiles.shape, F32),
        in_specs=[pl.BlockSpec(memory_space=pl.ANY)] * 4 + [vmem],
        out_specs=vmem,
        scratch_shapes=[
            pltpu.VMEM(same_keep.shape, BF16),
            pltpu.VMEM(cross_keep.shape, BF16),
            pltpu.SemaphoreType.DMA((2,)),
            pltpu.VMEM((count,) + tile, F32),
            pltpu.VMEM((count,) + tile, BF16),
            pltpu.VMEM((2 * count,) + tile, BF16),
            pltpu.VMEM((count,) + part, F32),
            pltpu.VMEM((count,) + part, BF16),
            pltpu.VMEM((count, rows, rows), BF16),
            pltpu.VMEM((count,) + part, BF16),
            pltpu.VMEM((count,) + part, BF16),
            pltpu.VMEM((count,) + part, BF16),
            pltpu.VMEM(part, BF16),
            pltpu.VMEM(part, BF16),
            pltpu.VMEM((rows, rows), F32),
            pltpu.SemaphoreType.DMA((2 * stages + 2,)),
            pltpu.SemaphoreType.DMA((2 * stages + 2,)),
        ],
        compiler_params=pltpu.CompilerParams(
            collective_id=1, has_side_effects=True, vmem_limit_bytes=62 * 2**20
        ),
        name="reduce",
    )(same_keep, same_send, cross_keep, cross_send, target_tiles)


def gathered(slot, panel_blocks, hi, lo, columns):
    count, blocks, rows, width = panel_blocks.shape
    inverse = hi.astype(F32) + lo.astype(F32)
    solved = jnp.einsum("sjaw,swv->sjav", panel_blocks, inverse, precision=lax.Precision.HIGHEST)
    rounded = solved.astype(BF16)
    tiles = jnp.zeros((columns, rows, width), F32)
    for s in range(count):
        full = lax.all_gather(rounded[s], "row", axis=1, tiled=True)
        products = jnp.einsum("jaw,jbw->jab", rounded[s], full, preferred_element_type=F32)
        tiles = tiles.at[slot[s]].add(products)
    return solved, tiles


def on_device(columns, halves, diag_blocks, panel_blocks, ancestors, target_ids, target_tiles):
    me, half = lax.axis_index("col"), lax.axis_index("row")
    paired = halves == 2 and panel_blocks.shape[0] == 2 and panel_blocks.shape[2] == 2 * NB
    swap = [(0, 1), (1, 0)]
    if paired:
        outgoing = lax.dynamic_index_in_dim(panel_blocks, 1 - half, 0, keepdims=False).astype(BF16)
        other = lax.ppermute(outgoing, "row", swap)
    place = jnp.arange(columns, dtype=jnp.int32)
    if paired:
        near_ids = ids_by_distance(target_ids, columns)
        matches = ancestors[:, :, None] == near_ids[None, None, :]
        distance = jnp.sum(jnp.where(matches, place[None, None, :], 0), axis=2)
    else:
        all_ids = lax.all_gather(target_ids, "col", axis=0, tiled=True)
        matches = ancestors[:, :, None] == all_ids[None, None, :]
        position = jnp.sum(jnp.where(matches, place[None, None, :], 0), axis=2)
        distance = (position ^ me).astype(jnp.int32)
    bits = list(range(columns.bit_length() - 1))
    slot = jnp.zeros_like(distance)
    for bit in bits:
        slot = slot * 2 + ((distance >> bit) & 1)
    hi, lo = inverse_factors(diag_blocks)
    if not paired:
        panel_factor, tiles = gathered(slot, panel_blocks, hi, lo, columns)
        keep, send = tiles[: columns // 2], tiles[columns // 2 :].astype(BF16)
        return (panel_factor, target_tiles - halve_and_add(keep, send, bits, columns)[None])
    mine = half.astype(jnp.int32).reshape(1)
    panel_factor, same_keep, same_send, cross_keep, cross_send = panel_products(
        slot, mine, panel_blocks, other, hi, lo, columns
    )
    updated = reduced(bits, same_keep, same_send, cross_keep, cross_send, target_tiles)
    return (panel_factor, updated)


def solution(mesh):
    in_specs = (
        P("col", None, None),
        P("col", None, "row", None),
        P("col", None),
        P("col"),
        P("col", "row", None),
    )
    out_specs = (P("col", None, "row", None), P("col", "row", None))
    return jax.shard_map(
        functools.partial(on_device, mesh.shape["col"], mesh.shape["row"]),
        mesh=mesh,
        in_specs=in_specs,
        out_specs=out_specs,
        check_vma=False,
    )
```
